256 devices in a mesh: dp: 16 (over y, x_lo, core), cent: 16 (over x_hi, z).
Axes of the slice: x: 4 (x_hi: 2, x_lo: 2; x = x_hi * 2 + x_lo), y: 4, z: 8, core: 2. Of those that a mesh axis runs over, the one named last changes fastest.
Arguments:
- vectors: bfloat16 [524288, 1024], P(('dp', 'cent'))
- centroids: bfloat16 [1024, 1024], P('cent')
Outputs:
- updated: float32 [1024, 1024], P('cent', 'dp')
All inputs are finite; a program needn't handle non-finite values.
Results may differ from the reference program's by a relative error of at most 0.0011.
Values may be sent and summed in bfloat16 or wider, within the bound.
A program may use at most 64 MiB of HBM per device.

```python
import math
import jax
import jax.numpy as jnp
from jax import lax

W = 1024
K = 1024
NROWS = 524288


def shared_rows(key):
    return jax.random.normal(key, (K, W), jnp.float32)


def draw_centroids(key, part):
    basis = shared_rows(key)
    result = basis
    return result.astype(jnp.bfloat16)


def draw_vectors(key, part):
    key = jax.random.fold_in(key, 23)
    result = jax.random.normal(key, (NROWS, W), jnp.float32)
    return result.astype(jnp.bfloat16)


def setup_inputs(seed: int = 0) -> dict:
    key_list = jax.random.split(jax.random.key(seed), 3)
    return {
        "vectors": draw_vectors(jax.random.fold_in(key_list[2], 71), 0),
        "centroids": draw_centroids(jax.random.fold_in(key_list[2], 71), 0),
    }


def logit_block(vector_block, centroids):
    norms = lax.optimization_barrier(jnp.sum(centroids.astype(jnp.float32) ** 2, axis=1))
    cross = lax.dot_general(vector_block, centroids, (((1,), (1,)), ((), ())), preferred_element_type=jnp.float32)
    return (2.0 * cross - norms[None, :]) / math.sqrt(W)

def reference(vectors, centroids):
    row_block = math.gcd(NROWS, 4096)
    stacked = vectors.reshape(NROWS // row_block, row_block, W)

    def step_fn(running, vector_block):
        numerator, weight_sums = running
        logits = logit_block(vector_block, centroids)
        row_top = lax.optimization_barrier(jnp.max(logits, axis=1, keepdims=True))
        lse = row_top + jnp.log(lax.optimization_barrier(jnp.sum(jnp.exp(logits - row_top), axis=1, keepdims=True)))
        resp = jnp.exp(logits - lse).astype(jnp.bfloat16)
        numerator = numerator + jnp.dot(resp.T, vector_block, preferred_element_type=jnp.float32)
        weight_sums = weight_sums + lax.optimization_barrier(jnp.sum(resp.astype(jnp.float32), axis=0))
        return ((numerator, weight_sums), None)
    start_state = (jnp.zeros((K, W), jnp.float32), jnp.zeros((K,), jnp.float32))
    (numerator, weight_sums), unused = lax.scan(step_fn, start_state, stacked)
    return (numerator + centroids.astype(jnp.float32)) / (weight_sums[:, None] + 1.0)
```

```python
import functools
import math

import jax
import jax.numpy as jnp
from jax import lax
from jax.experimental import pallas as pl
from jax.experimental.pallas import tpu as pltpu
from jax.sharding import PartitionSpec as P

F32 = jnp.float32
BF16 = jnp.bfloat16
LOG2E = math.log2(math.e)
DZ = (0, 1, 7, 2, 6, 3, 5, 4)
NT = (((1,), (1,)), ((), ()))


def device(x, y, z, core):
    return {"dp": y * 4 + lax.rem(x, 2) * 2 + core, "cent": (x // 2) * 8 + z}


def kernel(
    vec_hbm, cen, out,
    vec, G, E, R, ms, ss, wp, NUM, SIB, RSIB, SB, RB, S2, R2, S3, R3,
    W0, W1, W2, WS, WA, WB, WZ,
    load_sem, gs, gr, fs, fr, hs, hr, cs, cr, a_s, a_r, b_s, b_r, zs, zr, ws, wr,
):
    dp, cent = lax.axis_index("dp"), lax.axis_index("cent")
    core = lax.rem(dp, 2)
    x_lo = lax.rem(dp // 2, 2)
    y = dp // 4
    xh = cent // 8
    z = lax.rem(cent, 8)
    x = xh * 2 + x_lo
    first = core == 0
    sibling = device(x, y, z, 1 - core)

    def on_x(j):
        return device(lax.rem(x + j, 4), y, z, core)

    def on_y(j):
        return device(x, lax.rem(y + j, 4), z, core)

    def on_z(j):
        return device(x, y, lax.rem(z + j, 8), core)

    def on_a(j):
        return device(lax.rem(x + j * core, 4), lax.rem(y + j * (1 - core), 4), z, core)

    def on_b(j):
        return device(lax.rem(x + j * (1 - core), 4), lax.rem(y + j * core, 4), z, core)

    load = pltpu.make_async_copy(vec_hbm, vec, load_sem)
    load.start()

    barrier = pltpu.get_barrier_semaphore()
    peers = [sibling]
    peers += [on_x(j) for j in (1, 2, 3)]
    peers += [on_y(j) for j in (1, 2, 3)]
    peers += [on_z(j) for j in range(1, 8)]
    for peer in peers:
        pl.semaphore_signal(barrier, inc=1, device_id=peer)

    h = x_lo + xh - 2 * x_lo * xh
    quarter = lax.rem(y + 2 * h, 4)
    cols = pl.ds(pl.multiple_of(core * 512, 512), 512)
    G[quarter, 0, xh, :, cols] = cen[pl.ds(pl.multiple_of(quarter * 16, 16), 16), cols]

    pl.semaphore_wait(barrier, len(peers))

    sent = []

    def send(src, dst, s, r, to):
        copy = pltpu.make_async_remote_copy(
            src_ref=src, dst_ref=dst, send_sem=s, recv_sem=r, device_id=to
        )
        copy.start()
        sent.append(copy)
        return copy

    across = device(3 - x, y, z, core)
    beside = device(x + 1 - 2 * x_lo, y, z, core)
    own = G.at[quarter, 0, xh, :, cols]
    to_across = send(own, own, gs.at[14], gr.at[14], across)
    ring = [
        send(own, G.at[quarter, s, xh, :, cols], gs.at[s - 1], gr.at[s - 1], on_z(8 - DZ[s]))
        for s in range(1, 8)
    ]
    to_across.wait_recv()
    other = G.at[quarter, 0, 1 - xh, :, cols]
    ring2 = [
        send(other, G.at[quarter, s, 1 - xh, :, cols], gs.at[6 + s], gr.at[6 + s], on_z(8 - DZ[s]))
        for s in range(1, 8)
    ]
    near = (on_y(1), on_y(3), beside, sibling)
    passed = []
    for s in range(8):
        if s:
            ring[s - 1].wait_recv()
            ring2[s - 1].wait_recv()
        piece = G.at[quarter, s, :, :, cols]
        passed.append(
            [send(piece, piece, fs.at[s * 4 + k], fr.at[s * 4 + k], near[k]) for k in range(4)]
        )

    def logits(q):
        g = G[q].reshape(256, 1024)
        gf = g.astype(F32)
        bias = jnp.sum(gf * gf, axis=1, keepdims=True) * (LOG2E / 32.0)

        def body(i, carry):
            for u in range(4):
                n = pl.ds(pl.multiple_of(i * 1024 + u * 256, 256), 256)
                cross = lax.dot_general(g, vec[n, :], NT, preferred_element_type=F32)
                logit = cross * (LOG2E / 16.0) - bias
                top = jnp.max(logit, axis=0, keepdims=True)
                e = jnp.exp2(logit - top)
                E[q, :, n] = e
                ms[q, :, n] = top
                ss[q, :, n] = jnp.sum(e, axis=0, keepdims=True)
            return carry

        lax.fori_loop(0, 2, body, 0)

    load.wait()
    for s in range(8):
        passed[s][3].wait_recv()
    logits(quarter)
    quarters = (lax.rem(quarter + 3, 4), lax.rem(quarter + 1, 4), lax.rem(quarter + 2, 4))
    over = []
    for k in range(3):
        for s in range(8):
            passed[s][k].wait_recv()
        piece = G.at[quarters[k], :, :, :, cols]
        over.append(send(piece, piece, hs.at[k], hr.at[k], sibling))
    for k in range(3):
        over[k].wait_recv()
        logits(quarters[k])

    tops = [ms[q] for q in range(4)]
    top = functools.reduce(jnp.maximum, tops)
    scales = [jnp.exp2(t - top) for t in tops]
    total = functools.reduce(jnp.add, [ss[q] * scales[q] for q in range(4)])
    for q in range(4):
        ms[q] = scales[q] / total

    def responsibilities(q, u):
        n = slice(u * 512, u * 512 + 512)
        r = (E[q, :, n] * ms[q, :, n]).astype(BF16)
        R[q, :, n] = r
        rf = r.astype(F32)
        part = rf[:, 0:128] + rf[:, 128:256] + rf[:, 256:384] + rf[:, 384:512]
        wp[q] = part if u == 0 else wp[q] + part

    lo = lax.broadcasted_iota(jnp.int32, (64, 128), 1) < 64

    def combine(q):
        to_sib[q].wait_recv()
        for xx in range(4):
            for yy in range(4):
                t = NUM[q, xx * 4 + yy] + RSIB[q, xx * 4 + yy]
                NUM[q, xx * 4 + yy] = t
                SB[q, jnp.where(first, yy, xx), jnp.where(first, xx, yy)] = t.astype(BF16)
        a = jnp.where(first, y, x)
        to_a.append(
            [
                send(SB.at[q, lax.rem(a + j, 4)], RB.at[q, j - 1], a_s.at[q * 3 + j - 1], a_r.at[q * 3 + j - 1], on_a(j))
                for j in (1, 2, 3)
            ]
        )

    to_sib, to_a = [], []
    for u in range(4):
        responsibilities(0, u)
    for q in range(4):
        for yy in range(4):
            d = jnp.dot(R[q], vec[:, yy * 256 : yy * 256 + 256], preferred_element_type=F32)
            if q < 3:
                responsibilities(q + 1, yy)
            d = d.reshape(8, 2, 2, 8, 256)
            for xx in range(4):
                lanes = slice((xx % 2) * 128, (xx % 2) * 128 + 128)
                top_rows = d[:, xx // 2, 0, :, lanes].reshape(64, 128)
                low_rows = d[:, xx // 2, 1, :, lanes].reshape(64, 128)
                p0 = jnp.where(lo, top_rows, pltpu.roll(low_rows, 64, 1))
                p1 = jnp.where(lo, pltpu.roll(top_rows, 64, 1), low_rows)
                NUM[q, xx * 4 + yy] = jnp.where(first, p0, p1)
                SIB[q, xx * 4 + yy] = jnp.where(first, p1, p0)
        to_sib.append(send(SIB.at[q], RSIB.at[q], cs.at[q], cr.at[q], sibling))
        if q >= 1:
            combine(q - 1)
        if q == 2:
            for k in range(8):
                block = wp[k // 2, (k % 2) * 128 : (k % 2) * 128 + 128, :]
                W0[k : k + 1, :] = jnp.sum(block.T, axis=0, keepdims=True)
            w_sib = send(W0, WS, ws.at[0], wr.at[0], sibling)
    w_sib.wait_recv()
    W1[...] = W0[...] + WS[...]
    w_a = [send(W1, WA.at[j - 1], ws.at[j], wr.at[j], on_a(j)) for j in (1, 2, 3)]
    combine(3)

    to_b = []
    b = jnp.where(first, x, y)
    for q in range(4):
        for j in range(3):
            to_a[q][j].wait_recv()
        for i in range(4):
            mine = NUM[q, jnp.where(first, i * 4 + y, x * 4 + i)]
            S2[q, i] = (
                mine + RB[q, 0, i].astype(F32) + RB[q, 1, i].astype(F32) + RB[q, 2, i].astype(F32)
            )
        to_b.append(
            [
                send(S2.at[q, lax.rem(b + j, 4)], R2.at[q, j - 1], b_s.at[q * 3 + j - 1], b_r.at[q * 3 + j - 1], on_b(j))
                for j in (1, 2, 3)
            ]
        )
        if q == 0:
            for j in range(3):
                w_a[j].wait_recv()
            W2[...] = W1[...] + WA[0] + WA[1] + WA[2]
            w_b = [send(W2, WB.at[j - 1], ws.at[3 + j], wr.at[3 + j], on_b(j)) for j in (1, 2, 3)]
    for j in range(3):
        w_b[j].wait_recv()
    W1b = W2[...] + WB[0] + WB[1] + WB[2]
    W0b = WS
    W0b[...] = W1b
    w_z = [send(W0b, WZ.at[s - 1], ws.at[6 + s], wr.at[6 + s], on_z(DZ[s])) for s in range(1, 8)]
    for q in range(4):
        for j in range(3):
            to_b[q][j].wait_recv()
        S3[q] = (S2[q, b] + R2[q, 0] + R2[q, 1] + R2[q, 2]).reshape(8, 8, 128)
    to_z = [
        send(S3.at[:, s], R3.at[s - 1], zs.at[s - 1], zr.at[s - 1], on_z(DZ[s])) for s in range(1, 8)
    ]
    for s in range(1, 8):
        w_z[s - 1].wait_recv()
    halves = [W0b[...], jnp.zeros((8, 128), F32)]
    for s in range(1, 8):
        w = WZ[s - 1]
        if s % 4:
            w = pltpu.roll(w, 128 - (s % 4) * 32, 1)
        halves[s // 4] = halves[s // 4] + w
    row = lax.broadcasted_iota(jnp.int32, (16, 128), 0)
    lane = lax.broadcasted_iota(jnp.int32, (16, 128), 1)
    mask = lane == row + xh * 16
    tile = pl.ds(pl.multiple_of((y * 2 + x_lo) * 128, 128), 128)
    block = cen[:, tile].astype(F32)
    block = jnp.where(first, block, pltpu.roll(block, 64, 1))
    for s in range(1, 8):
        to_z[s - 1].wait_recv()
    for q in range(4):
        w = halves[0][2 * q : 2 * q + 1, :] + halves[1][2 * q + 1 : 2 * q + 2, :]
        w = jnp.sum(jnp.where(mask, jnp.broadcast_to(w, (16, 128)), 0.0), axis=1, keepdims=True)
        f = S3[q, 0]
        for s in range(7):
            f = f + R3[s, q]
        rows = jnp.concatenate([f, pltpu.roll(f, 64, 1)], axis=0)
        res = (rows + block[q * 16 : q * 16 + 16]) / (w + 1.0)
        out[q * 16 : q * 16 + 16, :] = res[:, 0:64]
    for copy in sent:
        copy.wait_send()


def per_device(vectors, centroids):
    dma = pltpu.SemaphoreType.DMA
    vmem = pltpu.VMEM
    return pl.pallas_call(
        kernel,
        out_shape=jax.ShapeDtypeStruct((64, 64), F32),
        in_specs=[pl.BlockSpec(memory_space=pl.ANY), pl.BlockSpec(memory_space=pltpu.VMEM)],
        out_specs=pl.BlockSpec(memory_space=pltpu.VMEM),
        scratch_shapes=[
            vmem((2048, 1024), BF16),
            vmem((4, 8, 2, 16, 1024), BF16),
            vmem((4, 256, 2048), F32),
            vmem((4, 256, 2048), BF16),
            vmem((4, 1, 2048), F32),
            vmem((4, 1, 2048), F32),
            vmem((4, 256, 128), F32),
            vmem((4, 16, 64, 128), F32),
            vmem((4, 16, 64, 128), F32),
            vmem((4, 16, 64, 128), F32),
            vmem((4, 4, 4, 64, 128), BF16),
            vmem((4, 3, 4, 64, 128), BF16),
            vmem((4, 4, 64, 128), F32),
            vmem((4, 3, 64, 128), F32),
            vmem((4, 8, 8, 128), F32),
            vmem((7, 4, 8, 128), F32),
            vmem((8, 128), F32),
            vmem((8, 128), F32),
            vmem((8, 128), F32),
            vmem((8, 128), F32),
            vmem((3, 8, 128), F32),
            vmem((3, 8, 128), F32),
            vmem((7, 8, 128), F32),
            dma,
            dma((15,)), dma((15,)),
            dma((32,)), dma((32,)),
            dma((3,)), dma((3,)),
            dma((4,)), dma((4,)),
            dma((12,)), dma((12,)),
            dma((12,)), dma((12,)),
            dma((7,)), dma((7,)),
            dma((14,)), dma((14,)),
        ],
        compiler_params=pltpu.CompilerParams(
            collective_id=0, has_side_effects=True, vmem_limit_bytes=56 * 2**20
        ),
        name="step",
    )(vectors, centroids)


def solution(mesh):
    in_specs = (P(("dp", "cent"), None), P("cent", None))
    out_specs = P("cent", "dp")
    return jax.shard_map(
        per_device, mesh=mesh, in_specs=in_specs, out_specs=out_specs, check_vma=False
    )
```

```python
import functools
import math

import jax
import jax.numpy as jnp
from jax import lax
from jax.experimental import pallas as pl
from jax.experimental.pallas import tpu as pltpu
from jax.sharding import PartitionSpec as P

F32 = jnp.float32
BF16 = jnp.bfloat16
LOG2E = math.log2(math.e)
NT = (((1,), (1,)), ((), ()))


def device(x, y, z, core):
    return {"dp": y * 4 + lax.rem(x, 2) * 2 + core, "cent": (x // 2) * 8 + z}


def each(lo, hi, step):
    def body(i, carry):
        step(i)
        return carry

    lax.fori_loop(lo, hi, body, 0)


def kernel(
    vec_hbm, cen_hbm, out,
    vec, cen, G, E, R, ms, ss, wp, NUM, SIB, RSIB, SB, RB, S2, SB2, R2, S3, R3,
    W0, W1, W2, W3, WS, WA, WB, WZ,
    load_sem, gs, gr, fs, fr, hs, hr, cs, cr, a_s, a_r, b_s, b_r, zs, zr, ws, wr,
):
    dp, cent = lax.axis_index("dp"), lax.axis_index("cent")
    core = lax.rem(dp, 2)
    x_lo = lax.rem(dp // 2, 2)
    y = dp // 4
    xh = cent // 8
    z = lax.rem(cent, 8)
    x = xh * 2 + x_lo
    first = core == 0
    sibling = device(x, y, z, 1 - core)

    def on_x(j):
        return device(lax.rem(x + j, 4), y, z, core)

    def on_y(j):
        return device(x, lax.rem(y + j, 4), z, core)

    def on_z(j):
        return device(x, y, lax.rem(z + j, 8), core)

    def on_a(j):
        return device(lax.rem(x + j * core, 4), lax.rem(y + j * (1 - core), 4), z, core)

    def on_b(j):
        return device(lax.rem(x + j * (1 - core), 4), lax.rem(y + j * core, 4), z, core)

    def distance(s):
        return jnp.where(lax.rem(s, 2) == 1, (s + 1) // 2, 8 - s // 2)

    def remote(src, dst, s, r, n, to):
        return pltpu.make_async_remote_copy(
            src_ref=src, dst_ref=dst, send_sem=s.at[n], recv_sem=r.at[n], device_id=to
        )

    barrier = pltpu.get_barrier_semaphore()
    peers = [sibling]
    peers += [on_x(j) for j in (1, 2, 3)]
    peers += [on_y(j) for j in (1, 2, 3)]
    peers += [on_z(j) for j in range(1, 8)]
    for peer in peers:
        pl.semaphore_signal(barrier, inc=1, device_id=peer)

    h = x_lo + xh - 2 * x_lo * xh
    quarter = lax.rem(y + 2 * h, 4)
    cols = pl.ds(pl.multiple_of(core * 512, 512), 512)
    own = cen_hbm.at[pl.ds(pl.multiple_of(quarter * 16, 16), 16), cols]
    place = pltpu.make_async_copy(own, G.at[xh, quarter, 0, :, cols], load_sem.at[0])
    place.start()
    load = pltpu.make_async_copy(vec_hbm, vec, load_sem.at[1])
    load.start()
    load_cen = pltpu.make_async_copy(cen_hbm, cen, load_sem.at[2])
    load_cen.start()
    place.wait()

    pl.semaphore_wait(barrier, len(peers))

    across = device(3 - x, y, z, core)
    near = (on_y(1), on_y(3), device(x + 1 - 2 * x_lo, y, z, core), sibling)
    quarters = (lax.rem(quarter + 3, 4), lax.rem(quarter + 1, 4), lax.rem(quarter + 2, 4))

    def piece(c, q, s):
        return G.at[xh + c * (1 - 2 * xh), q, s, :, cols]

    def ring(s):
        return remote(piece(0, quarter, 0), piece(0, quarter, s), gs, gr, s, on_z(8 - distance(s)))

    def cross(s):
        p = piece(0, quarter, s)
        return remote(p, p, gs, gr, 8 + s, across)

    def give(c, s, k):
        p = piece(c, quarter, s)
        return remote(p, p, fs, fr, c * 32 + s * 4 + k, near[k])

    def over(c, s, k):
        p = piece(c, quarters[k], s)
        return remote(p, p, hs, hr, c * 24 + s * 3 + k, sibling)

    def hop(s):
        ring(s).wait_recv()
        cross(s).start()
        for k in range(4):
            give(0, s, k).start()

    def forward(s):
        cross(s).wait_recv()
        for k in range(4):
            give(1, s, k).start()

    def share(c, s):
        for k in range(3):
            give(c, s, k).wait_recv()
            over(c, s, k).start()

    def ready(c, s):
        give(c, s, 3).wait_recv()
        for k in range(3):
            over(c, s, k).wait_recv()

    share0 = functools.partial(share, 0)
    share1 = functools.partial(share, 1)

    each(1, 8, lambda s: ring(s).start())
    cross(0).start()
    for k in range(4):
        give(0, 0, k).start()
    each(1, 3, hop)
    forward(0)
    share0(0)
    each(3, 8, hop)
    each(1, 3, forward)
    each(1, 3, share0)
    share1(0)
    each(3, 5, forward)
    each(3, 5, share0)
    each(5, 8, forward)
    each(5, 8, share0)
    each(1, 3, share1)
    load.wait()

    def logits(p):
        c, s0 = p // 2, lax.rem(p, 2) * 4
        each(s0, s0 + 4, lambda s: ready(c, s))
        side = xh + c * (1 - 2 * xh)
        part = side * 2 + lax.rem(p, 2)
        gf = G[side, :, pl.ds(s0, 4)].reshape(256, 1024).astype(F32)
        bias = jnp.sum(gf * gf, axis=1, keepdims=True) * (LOG2E / 32.0)

        def tile(i):
            g = G[side, :, pl.ds(s0, 4)].reshape(256, 1024)
            for u in range(8):
                n = pl.ds(pl.multiple_of(i * 2048 + u * 256, 256), 256)
                dots = lax.dot_general(g, vec[n, :], NT, preferred_element_type=F32)
                logit = dots * (LOG2E / 16.0) - bias
                top = jnp.max(logit, axis=0, keepdims=True)
                e = jnp.exp2(logit - top)
                E[part, :, n] = e
                ms[part, :, n] = top
                ss[part, :, n] = jnp.sum(e, axis=0, keepdims=True)

        tile(0)
        each(jnp.where(p == 0, 3, jnp.where(p == 1, 5, 8)), jnp.where(p == 0, 5, 8), share1)

    each(0, 4, logits)

    tops = [ms[q] for q in range(4)]
    top = functools.reduce(jnp.maximum, tops)
    scales = [jnp.exp2(t - top) for t in tops]
    total = functools.reduce(jnp.add, [ss[q] * scales[q] for q in range(4)])
    for q in range(4):
        ms[q] = scales[q] / total

    def responsibilities(q, u):
        n = slice(u * 512, u * 512 + 512)
        for p in range(4):
            r = (E[p, q * 64 : q * 64 + 64, n] * ms[p, :, n]).astype(BF16)
            rows = slice(p * 64, p * 64 + 64)
            R[q, rows, n] = r
            rf = r.astype(F32)
            part = rf[:, 0:128] + rf[:, 128:256] + rf[:, 256:384] + rf[:, 384:512]
            wp[q, rows, :] = part if u == 0 else wp[q, rows, :] + part

    for u in range(4):
        responsibilities(0, u)

    def lane_sums(k):
        block = wp[k // 2, pl.ds(pl.multiple_of(lax.rem(k, 2) * 128, 128), 128), :]
        W0[pl.ds(k, 1), :] = jnp.sum(block.T, axis=0, keepdims=True)

    def w_sib():
        return remote(W0, WS, ws, wr, 0, sibling)

    def w_a(j):
        return remote(W1, WA.at[j - 1], ws, wr, j, on_a(j))

    def w_b(j):
        return remote(W2, WB.at[j - 1], ws, wr, 3 + j, on_b(j))

    def w_z(s):
        return remote(W3, WZ.at[s - 1], ws, wr, 6 + s, on_z(distance(s)))

    a = jnp.where(first, y, x)
    b = jnp.where(first, x, y)

    def to_sib(q):
        return remote(SIB.at[q], RSIB.at[q], cs, cr, q, sibling)

    def to_a(q, j):
        return remote(SB.at[q, lax.rem(a + j, 4)], RB.at[q, j - 1], a_s, a_r, q * 3 + j - 1, on_a(j))

    def to_b(q, j):
        return remote(SB2.at[q, lax.rem(b + j, 4)], R2.at[q, j - 1], b_s, b_r, q * 3 + j - 1, on_b(j))

    def to_z(i, s):
        part = pl.ds(3, 1) if i else pl.ds(0, 3)
        return remote(S3.at[part, s], R3.at[s - 1, part], zs, zr, i * 7 + s - 1, on_z(distance(s)))

    lo = lax.broadcasted_iota(jnp.int32, (64, 128), 1) < 64

    def combine(q):
        to_sib(q).wait_recv()

        def column(yy):
            for xx in range(4):
                t = NUM[q, xx * 4 + yy] + RSIB[q, yy, xx].astype(F32)
                NUM[q, xx * 4 + yy] = t
                SB[q, jnp.where(first, yy, xx), jnp.where(first, xx, yy)] = t.astype(BF16)

        each(0, 4, column)
        for j in (1, 2, 3):
            to_a(q, j).start()

    for q in range(4):
        for yy in range(4):
            d = jnp.dot(R[q], vec[:, yy * 256 : yy * 256 + 256], preferred_element_type=F32)
            if q < 3:
                responsibilities(q + 1, yy)
            d = d.reshape(2, 8, 2, 8, 256)
            for xx in range(4):
                lanes = slice((xx % 2) * 128, (xx % 2) * 128 + 128)
                top_rows = d[xx // 2, :, 0, :, lanes].reshape(64, 128)
                low_rows = d[xx // 2, :, 1, :, lanes].reshape(64, 128)
                p0 = jnp.where(lo, top_rows, pltpu.roll(low_rows, 64, 1))
                p1 = jnp.where(lo, pltpu.roll(top_rows, 64, 1), low_rows)
                NUM[q, xx * 4 + yy] = jnp.where(first, p0, p1)
                SIB[q, yy, xx] = jnp.where(first, p1, p0).astype(BF16)
        to_sib(q).start()
        if q >= 1:
            combine(q - 1)
    each(0, 8, lane_sums)
    w_sib().start()
    combine(3)
    w_sib().wait_recv()
    W1[...] = W0[...] + WS[...]
    for j in (1, 2, 3):
        w_a(j).start()

    def second(q):
        for j in (1, 2, 3):
            to_a(q, j).wait_recv()
        for i in range(4):
            t = NUM[q, jnp.where(first, i * 4 + y, x * 4 + i)]
            for j in range(3):
                t = t + RB[q, j, i].astype(F32)
            S2[q, i] = t
            SB2[q, i] = t.astype(BF16)
        for j in (1, 2, 3):
            to_b(q, j).start()

    def third(i):
        def collect(q):
            for j in (1, 2, 3):
                to_b(q, j).wait_recv()
            t = S2[q, b]
            for j in range(3):
                t = t + R2[q, j].astype(F32)
            S3[q] = t.reshape(8, 8, 128)

        each(3 if i else 0, 4 if i else 3, collect)
        each(1, 8, lambda s: to_z(i, s).start())

    each(0, 3, second)
    for j in (1, 2, 3):
        w_a(j).wait_recv()
    W2[...] = W1[...] + WA[0] + WA[1] + WA[2]
    for j in (1, 2, 3):
        w_b(j).start()
    second(3)
    third(0)
    for j in (1, 2, 3):
        w_b(j).wait_recv()
    W3[...] = W2[...] + WB[0] + WB[1] + WB[2]
    each(1, 8, lambda s: w_z(s).start())
    third(1)

    each(1, 8, lambda s: w_z(s).wait_recv())
    weights = W3[...]
    for s in range(1, 8):
        weights = weights + pltpu.roll(WZ[s - 1], 128 - s * 16, 1)
    row = lax.broadcasted_iota(jnp.int32, (16, 128), 0)
    lane = lax.broadcasted_iota(jnp.int32, (16, 128), 1)
    mask = lane == row
    tile = pl.ds(pl.multiple_of((y * 2 + x_lo) * 128, 128), 128)
    load_cen.wait()
    block = cen[:, tile].astype(F32)
    block = jnp.where(first, block, pltpu.roll(block, 64, 1))

    def arrived(s):
        to_z(0, s).wait_recv()
        to_z(1, s).wait_recv()

    each(1, 8, arrived)
    for q in range(4):
        w = jnp.where(xh == 0, weights[2 * q : 2 * q + 1, :], weights[2 * q + 1 : 2 * q + 2, :])
        w = jnp.sum(jnp.where(mask, jnp.broadcast_to(w, (16, 128)), 0.0), axis=1, keepdims=True)
        f = S3[q, 0]
        for s in range(7):
            f = f + R3[s, q]
        rows = jnp.concatenate([f, pltpu.roll(f, 64, 1)], axis=0)
        res = (rows + block[q * 16 : q * 16 + 16]) / (w + 1.0)
        out[q * 16 : q * 16 + 16, :] = res[:, 0:64]

    def sent_pieces(s):
        cross(s).wait_send()
        for c in range(2):
            for k in range(4):
                give(c, s, k).wait_send()
            for k in range(3):
                over(c, s, k).wait_send()

    def sent_sums(q):
        to_sib(q).wait_send()
        for j in (1, 2, 3):
            to_a(q, j).wait_send()
            to_b(q, j).wait_send()

    def sent_z(s):
        ring(s).wait_send()
        to_z(0, s).wait_send()
        to_z(1, s).wait_send()
        w_z(s).wait_send()

    each(0, 8, sent_pieces)
    each(0, 4, sent_sums)
    each(1, 8, sent_z)
    w_sib().wait_send()
    for j in (1, 2, 3):
        w_a(j).wait_send()
        w_b(j).wait_send()


def per_device(vectors, centroids):
    dma = pltpu.SemaphoreType.DMA
    vmem = pltpu.VMEM
    return pl.pallas_call(
        kernel,
        out_shape=jax.ShapeDtypeStruct((64, 64), F32),
        in_specs=[pl.BlockSpec(memory_space=pl.ANY)] * 2,
        out_specs=pl.BlockSpec(memory_space=pltpu.VMEM),
        scratch_shapes=[
            vmem((2048, 1024), BF16),
            vmem((64, 1024), BF16),
            vmem((2, 4, 8, 16, 1024), BF16),
            vmem((4, 256, 2048), F32),
            vmem((4, 256, 2048), BF16),
            vmem((4, 1, 2048), F32),
            vmem((4, 1, 2048), F32),
            vmem((4, 256, 128), F32),
            vmem((4, 16, 64, 128), F32),
            vmem((4, 4, 4, 64, 128), BF16),
            vmem((4, 4, 4, 64, 128), BF16),
            vmem((4, 4, 4, 64, 128), BF16),
            vmem((4, 3, 4, 64, 128), BF16),
            vmem((4, 4, 64, 128), F32),
            vmem((4, 4, 64, 128), BF16),
            vmem((4, 3, 64, 128), BF16),
            vmem((4, 8, 8, 128), F32),
            vmem((7, 4, 8, 128), F32),
            vmem((8, 128), F32),
            vmem((8, 128), F32),
            vmem((8, 128), F32),
            vmem((8, 128), F32),
            vmem((8, 128), F32),
            vmem((3, 8, 128), F32),
            vmem((3, 8, 128), F32),
            vmem((7, 8, 128), F32),
            dma((3,)),
            dma((16,)), dma((16,)),
            dma((64,)), dma((64,)),
            dma((48,)), dma((48,)),
            dma((4,)), dma((4,)),
            dma((12,)), dma((12,)),
            dma((12,)), dma((12,)),
            dma((14,)), dma((14,)),
            dma((14,)), dma((14,)),
        ],
        compiler_params=pltpu.CompilerParams(
            collective_id=0, has_side_effects=True, vmem_limit_bytes=56 * 2**20
        ),
        name="step",
    )(vectors, centroids)


def solution(mesh):
    in_specs = (P(("dp", "cent"), None), P("cent", None))
    out_specs = P("cent", "dp")
    return jax.shard_map(
        per_device, mesh=mesh, in_specs=in_specs, out_specs=out_specs, check_vma=False
    )
```

```python
import functools
import math

import jax
import jax.numpy as jnp
from jax import lax
from jax.experimental import pallas as pl
from jax.experimental.pallas import tpu as pltpu
from jax.sharding import PartitionSpec as P

F32 = jnp.float32
BF16 = jnp.bfloat16
LOG2E = math.log2(math.e)


def device(x, y, z, core):
    return {"dp": y * 4 + lax.rem(x, 2) * 2 + core, "cent": (x // 2) * 8 + z}


def each(lo, hi, step):
    def body(i, carry):
        step(i)
        return carry

    lax.fori_loop(lo, hi, body, 0)


def kernel(
    vec_hbm, cen_hbm, out,
    vec, vecT, cen, G, E, R, ms, ss, wp, NUM, SIB, RSIB, SB, RB, S2, SB2, R2, S3, R3,
    W0, W1, W2, W3, WS, WA, WB, WZ,
    load_sem, gs, gr, fs, fr, hs, hr, cs, cr, a_s, a_r, b_s, b_r, zs, zr, ws, wr,
):
    dp, cent = lax.axis_index("dp"), lax.axis_index("cent")
    core = lax.rem(dp, 2)
    x_lo = lax.rem(dp // 2, 2)
    y = dp // 4
    xh = cent // 8
    z = lax.rem(cent, 8)
    x = xh * 2 + x_lo
    first = core == 0
    sibling = device(x, y, z, 1 - core)

    def on_x(j):
        return device(lax.rem(x + j, 4), y, z, core)

    def on_y(j):
        return device(x, lax.rem(y + j, 4), z, core)

    def on_z(j):
        return device(x, y, lax.rem(z + j, 8), core)

    def on_a(j):
        return device(lax.rem(x + j * core, 4), lax.rem(y + j * (1 - core), 4), z, core)

    def on_b(j):
        return device(lax.rem(x + j * (1 - core), 4), lax.rem(y + j * core, 4), z, core)

    def distance(s):
        return jnp.where(lax.rem(s, 2) == 1, (s + 1) // 2, 8 - s // 2)

    def remote(src, dst, s, r, n, to):
        return pltpu.make_async_remote_copy(
            src_ref=src, dst_ref=dst, send_sem=s.at[n], recv_sem=r.at[n], device_id=to
        )

    barrier = pltpu.get_barrier_semaphore()
    peers = [sibling]
    peers += [on_x(j) for j in (1, 2, 3)]
    peers += [on_y(j) for j in (1, 2, 3)]
    peers += [on_z(j) for j in range(1, 8)]
    for peer in peers:
        pl.semaphore_signal(barrier, inc=1, device_id=peer)

    h = x_lo + xh - 2 * x_lo * xh
    quarter = lax.rem(y + 2 * h, 4)
    cols = pl.ds(pl.multiple_of(core * 512, 512), 512)
    own = cen_hbm.at[pl.ds(pl.multiple_of(quarter * 16, 16), 16), cols]
    place = pltpu.make_async_copy(own, G.at[xh, quarter, 0, :, cols], load_sem.at[0])
    place.start()
    load = pltpu.make_async_copy(vec_hbm, vec, load_sem.at[1])
    load.start()
    load_cen = pltpu.make_async_copy(cen_hbm, cen, load_sem.at[2])
    load_cen.start()
    place.wait()

    pl.semaphore_wait(barrier, len(peers))

    across = device(3 - x, y, z, core)
    near = (on_y(1), on_y(3), device(x + 1 - 2 * x_lo, y, z, core), sibling)
    quarters = (lax.rem(quarter + 3, 4), lax.rem(quarter + 1, 4), lax.rem(quarter + 2, 4))

    def piece(c, q, s):
        return G.at[xh + c * (1 - 2 * xh), q, s, :, cols]

    def ring(s):
        return remote(piece(0, quarter, 0), piece(0, quarter, s), gs, gr, s, on_z(8 - distance(s)))

    def cross(s):
        p = piece(0, quarter, s)
        return remote(p, p, gs, gr, 8 + s, across)

    def give(c, s, k):
        p = piece(c, quarter, s)
        return remote(p, p, fs, fr, c * 32 + s * 4 + k, near[k])

    def over(c, s, k):
        p = piece(c, quarters[k], s)
        return remote(p, p, hs, hr, c * 24 + s * 3 + k, sibling)

    def hop(s):
        ring(s).wait_recv()
        cross(s).start()
        for k in range(4):
            give(0, s, k).start()

    def forward(s):
        cross(s).wait_recv()
        for k in range(4):
            give(1, s, k).start()

    def share(c, s):
        for k in range(3):
            give(c, s, k).wait_recv()
            over(c, s, k).start()

    def ready(c, s):
        give(c, s, 3).wait_recv()
        for k in range(3):
            over(c, s, k).wait_recv()

    share0 = functools.partial(share, 0)
    share1 = functools.partial(share, 1)

    each(1, 8, lambda s: ring(s).start())
    cross(0).start()
    for k in range(4):
        give(0, 0, k).start()
    load.wait()

    def turn(i):
        n = pl.ds(pl.multiple_of(i * 256, 256), 256)
        vecT[:, n] = vec[n, :].T

    each(0, 8, turn)
    each(1, 3, hop)
    forward(0)
    each(3, 8, hop)
    share0(0)
    each(1, 3, forward)
    each(1, 3, share0)
    each(3, 5, forward)
    each(3, 5, share0)
    each(5, 8, forward)
    each(5, 8, share0)
    each(0, 3, share1)

    def logits(p):
        c, s0 = p // 2, lax.rem(p, 2) * 4
        each(s0, s0 + 4, lambda s: ready(c, s))
        side = xh + c * (1 - 2 * xh)
        part = side * 2 + lax.rem(p, 2)
        gf = G[side, :, pl.ds(s0, 4)].reshape(256, 1024).astype(F32)
        bias = jnp.sum(gf * gf, axis=1, keepdims=True) * (LOG2E / 32.0)

        def tile(i):
            g = G[side, :, pl.ds(s0, 4)].reshape(256, 1024)
            for u in range(8):
                n = pl.ds(pl.multiple_of(i * 2048 + u * 256, 256), 256)
                dots = jnp.dot(g, vecT[:, n], preferred_element_type=F32)
                logit = dots * (LOG2E / 16.0) - bias
                top = jnp.max(logit, axis=0, keepdims=True)
                e = jnp.exp2(logit - top)
                E[part, :, n] = e
                ms[part, :, n] = top
                ss[part, :, n] = jnp.sum(e, axis=0, keepdims=True)

        tile(0)
        each(jnp.where(p == 0, 3, jnp.where(p == 1, 5, 8)), jnp.where(p == 0, 5, 8), share1)

    each(0, 4, logits)

    tops = [ms[q] for q in range(4)]
    top = functools.reduce(jnp.maximum, tops)
    scales = [jnp.exp2(t - top) for t in tops]
    total = functools.reduce(jnp.add, [ss[q] * scales[q] for q in range(4)])
    for q in range(4):
        ms[q] = scales[q] / total

    def responsibilities(q, u):
        n = slice(u * 512, u * 512 + 512)
        for p in range(4):
            r = (E[p, q * 64 : q * 64 + 64, n] * ms[p, :, n]).astype(BF16)
            rows = slice(p * 64, p * 64 + 64)
            R[q, rows, n] = r
            rf = r.astype(F32)
            part = rf[:, 0:128] + rf[:, 128:256] + rf[:, 256:384] + rf[:, 384:512]
            wp[q, rows, :] = part if u == 0 else wp[q, rows, :] + part

    for u in range(4):
        responsibilities(0, u)

    def lane_sums(k):
        block = wp[k // 2, pl.ds(pl.multiple_of(lax.rem(k, 2) * 128, 128), 128), :]
        W0[pl.ds(k, 1), :] = jnp.sum(block.T, axis=0, keepdims=True)

    def w_sib():
        return remote(W0, WS, ws, wr, 0, sibling)

    def w_a(j):
        return remote(W1, WA.at[j - 1], ws, wr, j, on_a(j))

    def w_b(j):
        return remote(W2, WB.at[j - 1], ws, wr, 3 + j, on_b(j))

    def w_z(s):
        return remote(W3, WZ.at[s - 1], ws, wr, 6 + s, on_z(distance(s)))

    a = jnp.where(first, y, x)
    b = jnp.where(first, x, y)

    def to_sib(q):
        return remote(SIB.at[q], RSIB.at[q], cs, cr, q, sibling)

    def to_a(q, j):
        return remote(SB.at[q, lax.rem(a + j, 4)], RB.at[q, j - 1], a_s, a_r, q * 3 + j - 1, on_a(j))

    def to_b(q, j):
        return remote(SB2.at[q, lax.rem(b + j, 4)], R2.at[q, j - 1], b_s, b_r, q * 3 + j - 1, on_b(j))

    def to_z(i, s):
        part = pl.ds(3, 1) if i else pl.ds(0, 3)
        return remote(S3.at[part, s], R3.at[s - 1, part], zs, zr, i * 7 + s - 1, on_z(distance(s)))

    lo = lax.broadcasted_iota(jnp.int32, (64, 128), 1) < 64

    def combine(q):
        to_sib(q).wait_recv()

        def column(yy):
            for xx in range(4):
                t = NUM[q, xx * 4 + yy] + RSIB[q, yy, xx].astype(F32)
                NUM[q, xx * 4 + yy] = t
                SB[q, jnp.where(first, yy, xx), jnp.where(first, xx, yy)] = t.astype(BF16)

        each(0, 4, column)
        for j in (1, 2, 3):
            to_a(q, j).start()

    for q in range(4):
        for yy in range(4):
            d = jnp.dot(R[q], vec[:, yy * 256 : yy * 256 + 256], preferred_element_type=F32)
            if q < 3:
                responsibilities(q + 1, yy)
            d = d.reshape(2, 8, 2, 8, 256)
            for xx in range(4):
                lanes = slice((xx % 2) * 128, (xx % 2) * 128 + 128)
                top_rows = d[xx // 2, :, 0, :, lanes].reshape(64, 128)
                low_rows = d[xx // 2, :, 1, :, lanes].reshape(64, 128)
                p0 = jnp.where(lo, top_rows, pltpu.roll(low_rows, 64, 1))
                p1 = jnp.where(lo, pltpu.roll(top_rows, 64, 1), low_rows)
                NUM[q, xx * 4 + yy] = jnp.where(first, p0, p1)
                SIB[q, yy, xx] = jnp.where(first, p1, p0).astype(BF16)
        to_sib(q).start()
        if q >= 1:
            combine(q - 1)
    each(0, 8, lane_sums)
    w_sib().start()
    combine(3)
    w_sib().wait_recv()
    W1[...] = W0[...] + WS[...]
    for j in (1, 2, 3):
        w_a(j).start()

    def second(q):
        for j in (1, 2, 3):
            to_a(q, j).wait_recv()
        for i in range(4):
            t = NUM[q, jnp.where(first, i * 4 + y, x * 4 + i)]
            for j in range(3):
                t = t + RB[q, j, i].astype(F32)
            S2[q, i] = t
            SB2[q, i] = t.astype(BF16)
        for j in (1, 2, 3):
            to_b(q, j).start()

    def third(i):
        def collect(q):
            for j in (1, 2, 3):
                to_b(q, j).wait_recv()
            t = S2[q, b]
            for j in range(3):
                t = t + R2[q, j].astype(F32)
            S3[q] = t.reshape(8, 8, 128)

        each(3 if i else 0, 4 if i else 3, collect)
        each(1, 8, lambda s: to_z(i, s).start())

    def sent_pieces(s):
        cross(s).wait_send()
        for c in range(2):
            for k in range(4):
                give(c, s, k).wait_send()
            for k in range(3):
                over(c, s, k).wait_send()

    each(0, 8, sent_pieces)
    each(1, 8, lambda s: ring(s).wait_send())
    each(0, 4, lambda q: to_sib(q).wait_send())
    w_sib().wait_send()
    each(0, 3, second)
    for j in (1, 2, 3):
        w_a(j).wait_recv()
    W2[...] = W1[...] + WA[0] + WA[1] + WA[2]
    for j in (1, 2, 3):
        w_b(j).start()
    second(3)
    third(0)

    def sent_a(q):
        for j in (1, 2, 3):
            to_a(q, j).wait_send()

    def sent_b(q):
        for j in (1, 2, 3):
            to_b(q, j).wait_send()

    each(0, 4, sent_a)
    each(0, 3, sent_b)
    for j in (1, 2, 3):
        w_a(j).wait_send()
    for j in (1, 2, 3):
        w_b(j).wait_recv()
    W3[...] = W2[...] + WB[0] + WB[1] + WB[2]
    each(1, 8, lambda s: w_z(s).start())
    third(1)

    each(1, 8, lambda s: w_z(s).wait_recv())
    weights = W3[...]
    for s in range(1, 8):
        weights = weights + pltpu.roll(WZ[s - 1], 128 - s * 16, 1)
    row = lax.broadcasted_iota(jnp.int32, (16, 128), 0)
    lane = lax.broadcasted_iota(jnp.int32, (16, 128), 1)
    mask = lane == row
    tile = pl.ds(pl.multiple_of((y * 2 + x_lo) * 128, 128), 128)
    load_cen.wait()
    block = cen[:, tile].astype(F32)
    block = jnp.where(first, block, pltpu.roll(block, 64, 1))

    divisors = []
    for q in range(4):
        w = jnp.where(xh == 0, weights[2 * q : 2 * q + 1, :], weights[2 * q + 1 : 2 * q + 2, :])
        w = jnp.sum(jnp.where(mask, jnp.broadcast_to(w, (16, 128)), 0.0), axis=1, keepdims=True)
        divisors.append(w + 1.0)

    def arrived(s):
        to_z(0, s).wait_recv()
        to_z(1, s).wait_recv()

    each(1, 8, arrived)
    for q in range(4):
        f = S3[q, 0]
        for s in range(7):
            f = f + R3[s, q]
        rows = jnp.concatenate([f, pltpu.roll(f, 64, 1)], axis=0)
        res = (rows + block[q * 16 : q * 16 + 16]) / divisors[q]
        out[q * 16 : q * 16 + 16, :] = res[:, 0:64]

    def sent_z(s):
        to_z(0, s).wait_send()
        to_z(1, s).wait_send()
        w_z(s).wait_send()

    each(1, 8, sent_z)
    for j in (1, 2, 3):
        to_b(3, j).wait_send()
        w_b(j).wait_send()


def per_device(vectors, centroids):
    dma = pltpu.SemaphoreType.DMA
    vmem = pltpu.VMEM
    return pl.pallas_call(
        kernel,
        out_shape=jax.ShapeDtypeStruct((64, 64), F32),
        in_specs=[pl.BlockSpec(memory_space=pl.ANY)] * 2,
        out_specs=pl.BlockSpec(memory_space=pltpu.VMEM),
        scratch_shapes=[
            vmem((2048, 1024), BF16),
            vmem((1024, 2048), BF16),
            vmem((64, 1024), BF16),
            vmem((2, 4, 8, 16, 1024), BF16),
            vmem((4, 256, 2048), F32),
            vmem((4, 256, 2048), BF16),
            vmem((4, 1, 2048), F32),
            vmem((4, 1, 2048), F32),
            vmem((4, 256, 128), F32),
            vmem((4, 16, 64, 128), F32),
            vmem((4, 4, 4, 64, 128), BF16),
            vmem((4, 4, 4, 64, 128), BF16),
            vmem((4, 4, 4, 64, 128), BF16),
            vmem((4, 3, 4, 64, 128), BF16),
            vmem((4, 4, 64, 128), F32),
            vmem((4, 4, 64, 128), BF16),
            vmem((4, 3, 64, 128), BF16),
            vmem((4, 8, 8, 128), F32),
            vmem((7, 4, 8, 128), F32),
            vmem((8, 128), F32),
            vmem((8, 128), F32),
            vmem((8, 128), F32),
            vmem((8, 128), F32),
            vmem((8, 128), F32),
            vmem((3, 8, 128), F32),
            vmem((3, 8, 128), F32),
            vmem((7, 8, 128), F32),
            dma((3,)),
            dma((16,)), dma((16,)),
            dma((64,)), dma((64,)),
            dma((48,)), dma((48,)),
            dma((4,)), dma((4,)),
            dma((12,)), dma((12,)),
            dma((12,)), dma((12,)),
            dma((14,)), dma((14,)),
            dma((14,)), dma((14,)),
        ],
        compiler_params=pltpu.CompilerParams(
            collective_id=0, has_side_effects=True, vmem_limit_bytes=56 * 2**20
        ),
        name="step",
    )(vectors, centroids)


def solution(mesh):
    in_specs = (P(("dp", "cent"), None), P("cent", None))
    out_specs = P("cent", "dp")
    return jax.shard_map(
        per_device, mesh=mesh, in_specs=in_specs, out_specs=out_specs, check_vma=False
    )
```

```python
import functools
import math

import jax
import jax.numpy as jnp
from jax import lax
from jax.experimental import pallas as pl
from jax.experimental.pallas import tpu as pltpu
from jax.sharding import PartitionSpec as P

F32 = jnp.float32
BF16 = jnp.bfloat16
LOG2E = math.log2(math.e)


def device(x, y, z, core):
    return {"dp": y * 4 + lax.rem(x, 2) * 2 + core, "cent": (x // 2) * 8 + z}


def each(lo, hi, step):
    def body(i, carry):
        step(i)
        return carry

    lax.fori_loop(lo, hi, body, 0)


def kernel(
    vec_hbm, cen_hbm, out,
    vec, vecT, cen, G, E, R, ms, ss, wp, NUM, SIB, RSIB, SB, RB, S2, SB2, R2, S3, R3,
    W0, W1, W2, W3, WS, WA, WB, WZ,
    load_sem, gs, gr, fs, fr, hs, hr, cs, cr, a_s, a_r, b_s, b_r, zs, zr, ws, wr,
):
    dp, cent = lax.axis_index("dp"), lax.axis_index("cent")
    core = lax.rem(dp, 2)
    x_lo = lax.rem(dp // 2, 2)
    y = dp // 4
    xh = cent // 8
    z = lax.rem(cent, 8)
    x = xh * 2 + x_lo
    first = core == 0
    sibling = device(x, y, z, 1 - core)

    def on_x(j):
        return device(lax.rem(x + j, 4), y, z, core)

    def on_y(j):
        return device(x, lax.rem(y + j, 4), z, core)

    def on_z(j):
        return device(x, y, lax.rem(z + j, 8), core)

    def on_a(j):
        return device(lax.rem(x + j * core, 4), lax.rem(y + j * (1 - core), 4), z, core)

    def on_b(j):
        return device(lax.rem(x + j * (1 - core), 4), lax.rem(y + j * core, 4), z, core)

    def distance(s):
        return jnp.where(lax.rem(s, 2) == 1, (s + 1) // 2, 8 - s // 2)

    def remote(src, dst, s, r, n, to):
        return pltpu.make_async_remote_copy(
            src_ref=src, dst_ref=dst, send_sem=s.at[n], recv_sem=r.at[n], device_id=to
        )

    barrier = pltpu.get_barrier_semaphore()
    peers = [sibling]
    peers += [on_x(j) for j in (1, 2, 3)]
    peers += [on_y(j) for j in (1, 2, 3)]
    peers += [on_z(j) for j in range(1, 8)]
    for peer in peers:
        pl.semaphore_signal(barrier, inc=1, device_id=peer)

    h = x_lo + xh - 2 * x_lo * xh
    quarter = lax.rem(y + 2 * h, 4)
    cols = pl.ds(pl.multiple_of(core * 512, 512), 512)
    own = cen_hbm.at[pl.ds(pl.multiple_of(quarter * 16, 16), 16), cols]
    place = pltpu.make_async_copy(own, G.at[xh, quarter, 0, :, cols], load_sem.at[0])
    place.start()
    load = pltpu.make_async_copy(vec_hbm, vec, load_sem.at[1])
    load.start()
    load_cen = pltpu.make_async_copy(cen_hbm, cen, load_sem.at[2])
    load_cen.start()
    place.wait()

    pl.semaphore_wait(barrier, len(peers))

    across = device(3 - x, y, z, core)
    near = (on_y(1), on_y(3), device(x + 1 - 2 * x_lo, y, z, core), sibling)
    quarters = (lax.rem(quarter + 3, 4), lax.rem(quarter + 1, 4), lax.rem(quarter + 2, 4))

    def piece(c, q, s):
        return G.at[xh + c * (1 - 2 * xh), q, s, :, cols]

    def ring(s):
        return remote(piece(0, quarter, 0), piece(0, quarter, s), gs, gr, s, on_z(8 - distance(s)))

    def cross(s):
        p = piece(0, quarter, s)
        return remote(p, p, gs, gr, 8 + s, across)

    def give(c, s, k):
        p = piece(c, quarter, s)
        return remote(p, p, fs, fr, c * 32 + s * 4 + k, near[k])

    def over(c, s, k):
        p = piece(c, quarters[k], s)
        return remote(p, p, hs, hr, c * 24 + s * 3 + k, sibling)

    def hop(s):
        ring(s).wait_recv()
        cross(s).start()
        for k in range(4):
            give(0, s, k).start()

    def forward(s):
        cross(s).wait_recv()
        for k in range(4):
            give(1, s, k).start()

    def share(c, s):
        for k in range(3):
            give(c, s, k).wait_recv()
            over(c, s, k).start()

    def ready(c, s):
        give(c, s, 3).wait_recv()
        for k in range(3):
            over(c, s, k).wait_recv()

    share0 = functools.partial(share, 0)
    share1 = functools.partial(share, 1)

    each(1, 8, lambda s: ring(s).start())
    cross(0).start()
    for k in range(4):
        give(0, 0, k).start()
    load.wait()

    def turn(i):
        n = pl.ds(pl.multiple_of(i * 256, 256), 256)
        vecT[:, n] = vec[n, :].T

    each(0, 8, turn)
    each(1, 3, hop)
    forward(0)
    each(3, 8, hop)
    share0(0)
    each(1, 3, forward)
    each(1, 3, share0)
    each(3, 5, forward)
    each(3, 5, share0)
    each(5, 8, forward)
    each(5, 8, share0)
    each(0, 3, share1)

    def logits(p):
        c, s0 = p // 2, lax.rem(p, 2) * 4
        each(s0, s0 + 4, lambda s: ready(c, s))
        side = xh + c * (1 - 2 * xh)
        part = side * 2 + lax.rem(p, 2)
        gf = G[side, :, pl.ds(s0, 4)].reshape(256, 1024).astype(F32)
        bias = jnp.sum(gf * gf, axis=1, keepdims=True) * (LOG2E / 32.0)

        def tile(i):
            g = G[side, :, pl.ds(s0, 4)].reshape(256, 1024)
            for u in range(8):
                n = pl.ds(pl.multiple_of(i * 2048 + u * 256, 256), 256)
                dots = jnp.dot(g, vecT[:, n], preferred_element_type=F32)
                logit = dots * (LOG2E / 16.0) - bias
                top = jnp.max(logit, axis=0, keepdims=True)
                e = jnp.exp2(logit - top)
                E[part, :, n] = e
                ms[part, :, n] = top
                ss[part, :, n] = jnp.sum(e, axis=0, keepdims=True)

        tile(0)
        each(jnp.where(p == 0, 3, jnp.where(p == 1, 5, 8)), jnp.where(p == 0, 5, 8), share1)

    each(0, 4, logits)

    tops = [ms[q] for q in range(4)]
    top = functools.reduce(jnp.maximum, tops)
    scales = [jnp.exp2(t - top) for t in tops]
    total = functools.reduce(jnp.add, [ss[q] * scales[q] for q in range(4)])
    for q in range(4):
        ms[q] = scales[q] / total

    def responsibilities(q, u):
        n = slice(u * 512, u * 512 + 512)
        for p in range(4):
            r = (E[p, q * 64 : q * 64 + 64, n] * ms[p, :, n]).astype(BF16)
            rows = slice(p * 64, p * 64 + 64)
            R[q, rows, n] = r
            rf = r.astype(F32)
            part = rf[:, 0:128] + rf[:, 128:256] + rf[:, 256:384] + rf[:, 384:512]
            wp[q, rows, :] = part if u == 0 else wp[q, rows, :] + part

    for u in range(4):
        responsibilities(0, u)

    def lane_sums(k):
        block = wp[k // 2, pl.ds(pl.multiple_of(lax.rem(k, 2) * 128, 128), 128), :]
        W0[pl.ds(k, 1), :] = jnp.sum(block.T, axis=0, keepdims=True)

    def w_sib():
        return remote(W0, WS, ws, wr, 0, sibling)

    def w_a(j):
        return remote(W1, WA.at[j - 1], ws, wr, j, on_a(j))

    def w_b(j):
        return remote(W2, WB.at[j - 1], ws, wr, 3 + j, on_b(j))

    def w_z(s):
        return remote(W3, WZ.at[s - 1], ws, wr, 6 + s, on_z(distance(s)))

    a = jnp.where(first, y, x)
    b = jnp.where(first, x, y)

    def to_sib(q):
        return remote(SIB.at[q], RSIB.at[q], cs, cr, q, sibling)

    def to_a(q, j):
        return remote(SB.at[q, lax.rem(a + j, 4)], RB.at[q, j - 1], a_s, a_r, q * 3 + j - 1, on_a(j))

    def to_b(q, j):
        return remote(SB2.at[q, lax.rem(b + j, 4)], R2.at[q, j - 1], b_s, b_r, q * 3 + j - 1, on_b(j))

    def to_z(i, s):
        part = pl.ds(3, 1) if i else pl.ds(0, 3)
        return remote(S3.at[part, s], R3.at[s - 1, part], zs, zr, i * 7 + s - 1, on_z(distance(s)))

    lo = lax.broadcasted_iota(jnp.int32, (64, 128), 1) < 64

    def combine(q):
        to_sib(q).wait_recv()

        def column(yy):
            for xx in range(4):
                t = NUM[q, xx * 4 + yy] + RSIB[q, yy, xx].astype(F32)
                NUM[q, xx * 4 + yy] = t
                SB[q, jnp.where(first, yy, xx), jnp.where(first, xx, yy)] = t.astype(BF16)

        for yy in range(4):
            column(yy)
        for j in (2, 1, 3):
            to_a(q, j).start()

    for q in range(4):
        for yy in range(4):
            d = jnp.dot(R[q], vec[:, yy * 256 : yy * 256 + 256], preferred_element_type=F32)
            if q < 3:
                responsibilities(q + 1, yy)
            d = d.reshape(2, 8, 2, 8, 256)
            for xx in range(4):
                lanes = slice((xx % 2) * 128, (xx % 2) * 128 + 128)
                top_rows = d[xx // 2, :, 0, :, lanes].reshape(64, 128)
                low_rows = d[xx // 2, :, 1, :, lanes].reshape(64, 128)
                p0 = jnp.where(lo, top_rows, pltpu.roll(low_rows, 64, 1))
                p1 = jnp.where(lo, pltpu.roll(top_rows, 64, 1), low_rows)
                NUM[q, xx * 4 + yy] = jnp.where(first, p0, p1)
                SIB[q, yy, xx] = jnp.where(first, p1, p0).astype(BF16)
        to_sib(q).start()
        if q >= 1:
            combine(q - 1)
    each(0, 8, lane_sums)
    w_sib().start()
    combine(3)
    w_sib().wait_recv()
    W1[...] = W0[...] + WS[...]
    for j in (1, 2, 3):
        w_a(j).start()

    def second(q):
        for j in (1, 2, 3):
            to_a(q, j).wait_recv()
        for i in range(4):
            t = NUM[q, jnp.where(first, i * 4 + y, x * 4 + i)]
            for j in range(3):
                t = t + RB[q, j, i].astype(F32)
            S2[q, i] = t
            SB2[q, i] = t.astype(BF16)
        for j in (2, 1, 3):
            to_b(q, j).start()

    def third(i):
        def collect(q):
            for j in (1, 2, 3):
                to_b(q, j).wait_recv()
            t = S2[q, b]
            for j in range(3):
                t = t + R2[q, j].astype(F32)
            S3[q] = t.reshape(8, 8, 128)

        each(3 if i else 0, 4 if i else 3, collect)
        each(1, 8, lambda s: to_z(i, 8 - s).start())

    def sent_pieces(s):
        cross(s).wait_send()
        for c in range(2):
            for k in range(4):
                give(c, s, k).wait_send()
            for k in range(3):
                over(c, s, k).wait_send()

    each(0, 8, sent_pieces)
    each(1, 8, lambda s: ring(s).wait_send())
    each(0, 4, lambda q: to_sib(q).wait_send())
    w_sib().wait_send()
    each(0, 3, second)
    for j in (1, 2, 3):
        w_a(j).wait_recv()
    W2[...] = W1[...] + WA[0] + WA[1] + WA[2]
    for j in (1, 2, 3):
        w_b(j).start()
    second(3)
    third(0)

    def sent_a(q):
        for j in (1, 2, 3):
            to_a(q, j).wait_send()

    def sent_b(q):
        for j in (1, 2, 3):
            to_b(q, j).wait_send()

    each(0, 4, sent_a)
    each(0, 3, sent_b)
    for j in (1, 2, 3):
        w_a(j).wait_send()
    for j in (1, 2, 3):
        w_b(j).wait_recv()
    W3[...] = W2[...] + WB[0] + WB[1] + WB[2]
    each(1, 8, lambda s: w_z(s).start())
    third(1)

    each(1, 8, lambda s: w_z(s).wait_recv())
    weights = W3[...]
    for s in range(1, 8):
        weights = weights + pltpu.roll(WZ[s - 1], 128 - s * 16, 1)
    row = lax.broadcasted_iota(jnp.int32, (16, 128), 0)
    lane = lax.broadcasted_iota(jnp.int32, (16, 128), 1)
    mask = lane == row
    tile = pl.ds(pl.multiple_of((y * 2 + x_lo) * 128, 128), 128)
    load_cen.wait()
    block = cen[:, tile].astype(F32)
    block = jnp.where(first, block, pltpu.roll(block, 64, 1))

    divisors = []
    for q in range(4):
        w = jnp.where(xh == 0, weights[2 * q : 2 * q + 1, :], weights[2 * q + 1 : 2 * q + 2, :])
        w = jnp.sum(jnp.where(mask, jnp.broadcast_to(w, (16, 128)), 0.0), axis=1, keepdims=True)
        divisors.append(w + 1.0)

    def arrived(s):
        to_z(0, s).wait_recv()
        to_z(1, s).wait_recv()

    each(1, 8, arrived)
    for q in range(4):
        f = S3[q, 0]
        for s in range(7):
            f = f + R3[s, q]
        rows = jnp.concatenate([f, pltpu.roll(f, 64, 1)], axis=0)
        res = (rows + block[q * 16 : q * 16 + 16]) / divisors[q]
        out[q * 16 : q * 16 + 16, :] = res[:, 0:64]

    def sent_z(s):
        to_z(0, s).wait_send()
        to_z(1, s).wait_send()
        w_z(s).wait_send()

    each(1, 8, sent_z)
    for j in (1, 2, 3):
        to_b(3, j).wait_send()
        w_b(j).wait_send()


def per_device(vectors, centroids):
    dma = pltpu.SemaphoreType.DMA
    vmem = pltpu.VMEM
    return pl.pallas_call(
        kernel,
        out_shape=jax.ShapeDtypeStruct((64, 64), F32),
        in_specs=[pl.BlockSpec(memory_space=pl.ANY)] * 2,
        out_specs=pl.BlockSpec(memory_space=pltpu.VMEM),
        scratch_shapes=[
            vmem((2048, 1024), BF16),
            vmem((1024, 2048), BF16),
            vmem((64, 1024), BF16),
            vmem((2, 4, 8, 16, 1024), BF16),
            vmem((4, 256, 2048), F32),
            vmem((4, 256, 2048), BF16),
            vmem((4, 1, 2048), F32),
            vmem((4, 1, 2048), F32),
            vmem((4, 256, 128), F32),
            vmem((4, 16, 64, 128), F32),
            vmem((4, 4, 4, 64, 128), BF16),
            vmem((4, 4, 4, 64, 128), BF16),
            vmem((4, 4, 4, 64, 128), BF16),
            vmem((4, 3, 4, 64, 128), BF16),
            vmem((4, 4, 64, 128), F32),
            vmem((4, 4, 64, 128), BF16),
            vmem((4, 3, 64, 128), BF16),
            vmem((4, 8, 8, 128), F32),
            vmem((7, 4, 8, 128), F32),
            vmem((8, 128), F32),
            vmem((8, 128), F32),
            vmem((8, 128), F32),
            vmem((8, 128), F32),
            vmem((8, 128), F32),
            vmem((3, 8, 128), F32),
            vmem((3, 8, 128), F32),
            vmem((7, 8, 128), F32),
            dma((3,)),
            dma((16,)), dma((16,)),
            dma((64,)), dma((64,)),
            dma((48,)), dma((48,)),
            dma((4,)), dma((4,)),
            dma((12,)), dma((12,)),
            dma((12,)), dma((12,)),
            dma((14,)), dma((14,)),
            dma((14,)), dma((14,)),
        ],
        compiler_params=pltpu.CompilerParams(
            collective_id=0, has_side_effects=True, vmem_limit_bytes=56 * 2**20
        ),
        name="step",
    )(vectors, centroids)


def solution(mesh):
    in_specs = (P(("dp", "cent"), None), P("cent", None))
    out_specs = P("cent", "dp")
    return jax.shard_map(
        per_device, mesh=mesh, in_specs=in_specs, out_specs=out_specs, check_vma=False
    )
```
